32 devices in a mesh: batch: 2 (over y), rows: 8 (over z, x), cols: 2 (over core).
Axes of the slice: x: 2, y: 2, z: 4, core: 2. Of those that a mesh axis runs over, the one named last changes fastest.
Arguments:
- features: bfloat16 [8192, 1024], P(('batch', 'rows'), 'cols'), parts along dimension 0, may hold values from -6 to 6
- edge_vals: bfloat16 [64, 8, 128, 128], P(('batch', 'rows')), parts along dimension 0, may hold values from 0.019897461 to 1
- block_cols: int32 [64, 8], P(('batch', 'rows')), parts along dimension 0, may hold values from 0 to 31, as said below
- block_count: int32 [64], P(('batch', 'rows')), parts along dimension 0, may hold values from 1 to 8
- w_self: bfloat16 [1024, 1024], P('rows', 'cols'), may hold values from -0.1875 to 0.1875
- w_neigh: bfloat16 [1024, 1024], P('rows', 'cols'), may hold values from -3 to 3
- cotangent: bfloat16 [8192, 1024], P(('batch', 'rows'), 'cols'), parts along dimension 0, may hold values from -6 to 6
Outputs:
- output: bfloat16 [8192, 1024], P(('batch', 'rows'), 'cols'), parts along dimension 0
- grad_self: float32 [2048, 1024], P(('batch', 'rows'), 'cols'), parts along dimension 0
- grad_neigh: float32 [2048, 1024], P(('batch', 'rows'), 'cols'), parts along dimension 0
The draws below stay inside these ranges and needn't reach their ends.
There are 2 independent parts, one for each index of `batch`. The reference program is written for one: setup_inputs(seed, part) draws one part's arguments, and reference() takes and returns one part's arrays. A program takes and returns all parts, laid end to end along the dimension named above; an argument that names none is the same for every part. Nothing has to cross between parts.
Inputs may be any that keep to these rules, and one draw needn't show every extreme that they name: `block_cols`: each entry names a row block whose device along rows lies within 2 devices of the row block's own device; slot 0 names the row block itself.
All inputs are finite; a program needn't handle non-finite values.
Results may differ from the reference program's by a relative error of at most 0.0056.
Values may be sent and summed in bfloat16 or wider, within the bound.
A program may use at most 64 MiB of HBM per device.

```python
import math
import jax
import jax.numpy as jnp
from jax import lax

D = 1024
H = 1024
B = 128
K = 8
REACH = 2
BLK_DEV = 4
NBLK = 32
NODES = 4096
N_ROWS = 8


def draw_block_cols(key, part):
    key = jax.random.fold_in(key, 11)
    key_off, key_inner = jax.random.split(key)
    own = jnp.arange(NBLK, dtype=jnp.int32) // BLK_DEV
    offset = jax.random.randint(key_off, (NBLK, K), -REACH, REACH + 1, dtype=jnp.int32)
    device = jnp.clip(own[:, None] + offset, 0, N_ROWS - 1)
    inner = jax.random.randint(key_inner, (NBLK, K), 0, BLK_DEV, dtype=jnp.int32)
    cols = device * BLK_DEV + inner
    cols = cols.at[:, 0].set(jnp.arange(NBLK, dtype=jnp.int32))
    return cols.astype(jnp.int32)


def draw_block_count(key, part):
    key = jax.random.fold_in(key, 23)
    key_level, key_count, key_place = jax.random.split(key, 3)
    level = jax.random.randint(key_level, (N_ROWS,), 1, K + 1, dtype=jnp.int32)
    level = jnp.repeat(level, BLK_DEV)
    raw = jax.random.randint(key_count, (NBLK,), 0, 65536, dtype=jnp.int32)
    counts = 1 + raw % level
    place = jax.random.randint(key_place, (), 0, NBLK, dtype=jnp.int32)
    counts = counts.at[place].set(K)
    return counts.astype(jnp.int32)


def strengthened(array, rng, source, target, parts, factor):
    owner, partner = [(jnp.arange(array.shape[dim]) // (array.shape[dim] // parts)).reshape([-1 if axis == dim else 1 for axis in range(array.ndim)]) for dim in (source, target)]
    chosen = jax.random.permutation(rng, parts)[partner]
    strong = (owner == chosen) | (owner == (partner + parts // 2) % parts)
    return jnp.where(strong, factor * array, array)


def levels(key, dims, pieces, least, top_value):
    factor_of = 1.0
    for position, blocks in pieces:
        steps = jax.random.uniform(jax.random.fold_in(jax.random.fold_in(key, 6), position), (blocks,), jnp.float32, least / len(pieces), top_value / len(pieces))
        factor_of = factor_of * jnp.repeat(jnp.exp(steps), dims[position] // blocks).reshape((-1,) + (1,) * (len(dims) - 1 - position))
    return factor_of


def scatter_about(rng, shape, width, bound, shards=(), kind=jnp.bfloat16):
    loudness = levels(rng, shape, shards, -0.22, 0.18) if shards else 1.0
    array = jax.random.normal(rng, shape, jnp.float32) * width * loudness
    return jnp.minimum(jnp.maximum(array, -bound), bound).astype(kind)


def noise_with(rng, dims, width, most, cuts, heavy, held_as=jnp.bfloat16):
    values = width * jax.random.normal(rng, dims, jnp.float32)
    if cuts:
        values = values * levels(rng, dims, cuts, -0.22, 0.18)
    return jnp.clip(strengthened(values, jax.random.fold_in(rng, 3), *heavy), -most, most).astype(held_as)


def setup_inputs(seed: int = 0, part: int = 0) -> dict:
    splits = jax.random.split(jax.random.key(seed), 8)
    part_splits = jax.random.split(jax.random.fold_in(splits[7], part), 8)
    return {
        "features": noise_with(part_splits[0], (NODES, D), 1.0, 6.0, ((0, 8), (1, 2)), (0, 1, 8, 2.0)),
        "edge_vals": jnp.clip(jnp.exp(math.log(1.0) - 3.9171631 * jax.random.uniform(part_splits[1], (NBLK, K, B, B), jnp.float32) ** levels(part_splits[1], (NBLK, K, B, B), ((0, 8),), -0.2, 0.2)), 0.019897461, 1.0).astype(jnp.bfloat16),
        "block_cols": draw_block_cols(jax.random.fold_in(jax.random.fold_in(splits[7], part), 71), part),
        "block_count": draw_block_count(jax.random.fold_in(jax.random.fold_in(splits[7], part), 71), part),
        "w_self": scatter_about(splits[4], (D, H), D ** -0.5, 0.1875, ((0, 8), (1, 2))),
        "w_neigh": scatter_about(splits[5], (D, H), 4 ** -0.5, 3.0, ((0, 8), (1, 2))),
        "cotangent": scatter_about(part_splits[6], (NODES, H), 1.0, 6.0, ((0, 8), (1, 2))),
    }


def reference(features, edge_vals, block_cols, block_count, w_self, w_neigh, cotangent):
    feat_blocks = features.reshape(NBLK, B, D)

    def one_block(args):
        edges, cols, count = args
        used = jnp.arange(K) < count
        masked = jnp.where(used[:, None, None], edges, jnp.zeros_like(edges))
        blocks = feat_blocks[cols]
        acc = jnp.einsum('kij,kjf->if', masked.astype(jnp.float32), blocks.astype(jnp.float32))
        degree = lax.optimization_barrier(jnp.sum(masked.astype(jnp.float32), axis=(0, 2)))
        return (acc / degree[:, None]).astype(jnp.bfloat16)
    aggregated = lax.map(one_block, (edge_vals, block_cols, block_count)).reshape(NODES, D)
    pre = jnp.dot(features, w_self, preferred_element_type=jnp.float32)
    pre = pre + jnp.dot(aggregated, w_neigh, preferred_element_type=jnp.float32)
    sig = jax.nn.sigmoid(pre)
    output = (pre * sig).astype(jnp.bfloat16)
    grad_pre = (cotangent.astype(jnp.float32) * sig * (1.0 + pre * (1.0 - sig))).astype(jnp.bfloat16)
    inv = 1.0 / math.sqrt(NODES)
    grad_self = jnp.dot(features.T, grad_pre, preferred_element_type=jnp.float32) * inv
    grad_neigh = jnp.dot(aggregated.T, grad_pre, preferred_element_type=jnp.float32) * inv
    return (output, grad_self, grad_neigh)
```

```python
import functools
import math

import jax
import jax.numpy as jnp
from jax import lax
from jax.experimental import pallas as pl
from jax.experimental.pallas import tpu as pltpu
from jax.sharding import PartitionSpec as P

B = 128
REACH = 2
TILE = 128


def passed_along(array, axis, by):
    peers = lax.axis_size(axis)
    pairs = [(i, i + by) for i in range(peers) if 0 <= i + by < peers]
    return lax.ppermute(array, axis, pairs)


def local(features, edge_vals, block_cols, block_count, w_self, w_neigh, cotangent):
    node_rows = features.shape[0]
    width = features.shape[1]
    blocks_here = node_rows // B
    slot_count = edge_vals.shape[1]
    pieces_list = []
    for offset in range(-REACH, REACH + 1):
        if offset == 0:
            pieces_list.append(features)
        else:
            pieces_list.append(passed_along(features, "rows", -offset))
    extended = jnp.concatenate(pieces_list, axis=0)
    ext_blocks = extended.reshape(-1, B, width)
    base = (lax.axis_index("rows") - REACH) * blocks_here
    local_cols = block_cols - base
    used = jnp.arange(slot_count)[None, :] < block_count[:, None]
    masked = jnp.where(used[:, :, None, None], edge_vals, jnp.zeros_like(edge_vals))
    degree = jnp.sum(masked.astype(jnp.float32), axis=(1, 3))
    picked = ext_blocks[local_cols]
    summed = jnp.einsum("bkij,bkjf->bif", masked, picked, preferred_element_type=jnp.float32)
    aggregated = (summed / degree[:, :, None]).reshape(node_rows, width).astype(jnp.bfloat16)
    full_feat = lax.all_gather(features, "cols", axis=1, tiled=True)
    full_agg = lax.all_gather(aggregated, "cols", axis=1, tiled=True)

    def add_rows(left, piece):
        return jnp.dot(left, piece, preferred_element_type=jnp.float32)

    self_part = add_rows(full_feat, lax.all_gather(w_self, "rows", axis=0, tiled=True))
    neigh_part = add_rows(full_agg, lax.all_gather(w_neigh, "rows", axis=0, tiled=True))
    pre = self_part + neigh_part
    sigma = jax.nn.sigmoid(pre)
    output = (pre * sigma).astype(jnp.bfloat16)
    grad_pre = (cotangent.astype(jnp.float32) * sigma * (1.0 + pre * (1.0 - sigma))).astype(
        jnp.bfloat16
    )
    inverse = 1.0 / math.sqrt(node_rows * lax.axis_size("rows"))
    grads = lax.psum_scatter(
        jnp.concatenate(
            [
                jnp.einsum("nk,nh->kh", full_feat, grad_pre, preferred_element_type=jnp.float32),
                jnp.einsum("nk,nh->kh", full_agg, grad_pre, preferred_element_type=jnp.float32),
            ],
            axis=1,
        ),
        "rows",
        scatter_dimension=0,
        tiled=True,
    )
    out_cols = grad_pre.shape[1]
    grad_self = grads[:, :out_cols] * inverse
    grad_neigh = grads[:, out_cols:] * inverse
    return (output, grad_self, grad_neigh)


F32 = jnp.float32
BF16 = jnp.bfloat16


def dest_order(step, pair, pairs):
    above = pairs - 1 - pair
    low = jnp.where(step < above, pairs - 1 - step, step - above)
    high = jnp.where(step < pair, step, pairs - 1 - (step - pair))
    return jnp.where(step == pairs - 1, pair, jnp.where(2 * pair < pairs, low, high))


def layer(
    n, f_ref, e_ref, cols_ref, count_ref, ws_ref, wn_ref, cot_ref,
    out_ref, gs_ref, gn_ref,
    ext, full, agg, masked, inv_deg, w, gp, part, xs, xr, zs, zr,
    h_recv, h_x, h_z, h_relay, c_send, c_recv, w_recv, w_send,
    x_send, x_recv, z_send, z_recv,
):
    batch, row, col = lax.axis_index("batch"), lax.axis_index("rows"), lax.axis_index("cols")
    pairs = n // 2
    pair, side = row // 2, row % 2
    partner = row + 1 - 2 * side
    nodes, width = out_ref.shape[0], f_ref.shape[2]
    depth = ws_ref.shape[0]
    blocks, slots = e_ref.shape[0], e_ref.shape[1]
    half = blocks // 2
    has_up, has_down = pair < pairs - 1, pair > 0
    pending = []

    def remote(src, dst, send, recv, to):
        return pltpu.make_async_remote_copy(
            src_ref=src, dst_ref=dst, send_sem=send, recv_sem=recv,
            device_id=to, device_id_type=pl.DeviceIdType.MESH,
        )

    def send(cond, make):
        if cond is None:
            make().start()
        else:
            @pl.when(cond)
            def _():
                make().start()
        pending.append((cond, make))

    def arrived(dst, sem):
        remote(dst, dst, sem, sem, {"cols": 1 - col}).wait_recv()

    barrier = pltpu.get_barrier_semaphore()
    mesh_id = pl.DeviceIdType.MESH
    for to in ({"cols": 1 - col}, {"batch": 1 - batch}, {"rows": partner}):
        pl.semaphore_signal(barrier, inc=1, device_id=to, device_id_type=mesh_id)

    @pl.when(has_up)
    def _():
        pl.semaphore_signal(barrier, inc=1, device_id={"rows": row + 2}, device_id_type=mesh_id)

    @pl.when(has_down)
    def _():
        pl.semaphore_signal(barrier, inc=1, device_id={"rows": row - 2}, device_id_type=mesh_id)

    w[0, pl.ds(pl.multiple_of(row * depth, depth), depth), :] = ws_ref[...]
    w[1, pl.ds(pl.multiple_of(row * depth, depth), depth), :] = wn_ref[...]
    pl.semaphore_wait(barrier, 3 + has_up.astype(jnp.int32) + has_down.astype(jnp.int32))

    def shard(which, origin):
        return w.at[which, pl.ds(pl.multiple_of(origin * depth, depth), depth), :]

    def send_w(cond, way, origin, to):
        send(cond, lambda: remote(
            shard(batch, origin), shard(batch, origin),
            w_send.at[way, origin], w_recv.at[batch, origin], to))

    up, down = {"rows": row + 2}, {"rows": row - 2}
    send_w(has_up, 0, row, up)
    send_w(has_down, 1, row, down)
    send_w(None, 2, row, {"rows": partner})

    def rows_of(slot, piece):
        return ext.at[pl.ds(slot * blocks + piece * half, half)]

    partner_slot = 3 - 2 * side
    diag_slot = 1 + 2 * side
    far_slot = 4 - 4 * side
    for piece in (0, 1):
        send(None, lambda piece=piece: remote(
            f_ref.at[pl.ds(piece * half, half)], rows_of(diag_slot, piece),
            h_x.at[piece], h_recv.at[diag_slot, piece], {"rows": partner}))
        other = 1 - piece
        send(has_up, lambda piece=other: remote(
            f_ref.at[pl.ds(piece * half, half)], rows_of(0, piece),
            h_z.at[0, piece], h_recv.at[0, piece], up))
        send(has_down, lambda piece=other: remote(
            f_ref.at[pl.ds(piece * half, half)], rows_of(4, piece),
            h_z.at[1, piece], h_recv.at[4, piece], down))
    send(None, lambda: remote(
        f_ref, full.at[col], c_send.at[0], c_recv.at[0], {"cols": 1 - col}))

    ext[REACH * blocks:(REACH + 1) * blocks] = f_ref[...]
    full[col] = f_ref[...]

    def prepare(i, carry):
        degree = jnp.zeros((B, B), F32)
        for s in range(slots):
            keep = jnp.clip(count_ref[i] - s, 0, 1).astype(F32)
            edge = e_ref[i, s].astype(F32) * keep
            masked[i, :, s * B:(s + 1) * B] = edge.astype(BF16)
            degree = degree + edge
        total = jnp.sum(degree, axis=1, keepdims=True)
        inv_deg[i] = jnp.broadcast_to(1.0 / total, (B, B))
        return carry

    lax.fori_loop(0, blocks, prepare, 0)

    def forward(origin, cond, along, way, to):
        @pl.when(cond)
        def _():
            arrived(shard(batch, origin), w_recv.at[batch, origin])
        send_w(cond & along, way, origin, to)
        send_w(cond, 2, origin, {"rows": partner})
        send_w(cond, 3, origin, {"batch": 1 - batch})

    def hand_over(origin, cond):
        def wait():
            arrived(shard(batch, origin), w_recv.at[batch, origin])
        if cond is None:
            wait()
        else:
            pl.when(cond)(wait)
        send_w(cond, 3, origin, {"batch": 1 - batch})

    has_far = jnp.where(side == 0, has_up.astype(jnp.int32), has_down.astype(jnp.int32)) == 1
    has_diag = jnp.where(side == 0, has_down.astype(jnp.int32), has_up.astype(jnp.int32)) == 1
    far = row + 2 - 4 * side
    hand_over(partner, None)
    for hop in range(1, pairs):
        below, above = pair >= hop, pair + hop < pairs
        forward(row - 2 * hop, below, has_up, 0, up)
        forward(row + 2 * hop, above, has_down, 1, down)
        if hop == 1:
            arrived(rows_of(partner_slot, 0), h_recv.at[partner_slot, 0])
            send(has_far, lambda: remote(
                rows_of(partner_slot, 0), rows_of(diag_slot, 0),
                h_relay.at[0], h_recv.at[diag_slot, 0], {"rows": far}))

            @pl.when(has_far)
            def _():
                arrived(rows_of(far_slot, 1), h_recv.at[far_slot, 1])
            send(has_far, lambda: remote(
                rows_of(far_slot, 1), rows_of(partner_slot, 1),
                h_relay.at[1], h_recv.at[partner_slot, 1], {"rows": partner}))
        hand_over(partner - 2 * hop, below)
        hand_over(partner + 2 * hop, above)

    arrived(rows_of(partner_slot, 1), h_recv.at[partner_slot, 1])

    @pl.when(has_far)
    def _():
        arrived(rows_of(far_slot, 0), h_recv.at[far_slot, 0])

    @pl.when(has_diag)
    def _():
        for piece in (0, 1):
            arrived(rows_of(4 - far_slot, piece), h_recv.at[4 - far_slot, piece])
            arrived(rows_of(diag_slot, piece), h_recv.at[diag_slot, piece])

    first = (row - REACH) * blocks

    def aggregate(i, carry):
        acc = jnp.zeros((B, width), F32)
        for s in range(0, slots, 2):
            picked = []
            for k in (s, s + 1):
                picked.append(ext[jnp.clip(cols_ref[i, k] - first, 0, ext.shape[0] - 1)])
            acc = acc + jnp.dot(
                masked[i, :, s * B:(s + 2) * B], jnp.concatenate(picked, axis=0),
                preferred_element_type=F32)
        agg[col, i] = (acc * inv_deg[i, :, 0:1]).astype(BF16)
        return carry

    lax.fori_loop(0, blocks, aggregate, 0)
    send(None, lambda: remote(
        agg.at[col], agg.at[col], c_send.at[1], c_recv.at[1], {"cols": 1 - col}))

    arrived(full.at[1 - col], c_recv.at[0])

    def handed_over(cond, origin):
        def wait():
            arrived(shard(1 - batch, origin), w_recv.at[1 - batch, origin])
        if cond is None:
            wait()
        else:
            pl.when(cond)(wait)

    handed_over(None, partner)
    for hop in range(1, pairs):
        for origin in (row, partner):
            handed_over(pair >= hop, origin - 2 * hop)
            handed_over(pair + hop < pairs, origin + 2 * hop)
    arrived(agg.at[1 - col], c_recv.at[1])

    span = 2
    tile = span * B

    def left(array, h, i):
        return array[h, pl.ds(i * span, span)].reshape(tile, width)

    def activate(i, carry):
        at = pl.ds(pl.multiple_of(i * tile, tile), tile)
        pre = jnp.zeros((tile, w.shape[2]), F32)
        for h in (0, 1):
            pre = pre + jnp.dot(left(full, h, i), w[0, h * width:(h + 1) * width, :], preferred_element_type=F32)
            pre = pre + jnp.dot(left(agg, h, i), w[1, h * width:(h + 1) * width, :], preferred_element_type=F32)
        sigma = jax.nn.sigmoid(pre)
        out_ref[at, :] = (pre * sigma).astype(BF16)
        gp[at, :] = (cot_ref[at, :].astype(F32) * sigma * (1.0 + pre * (1.0 - sigma))).astype(BF16)
        return carry

    lax.fori_loop(0, nodes // tile, activate, 0)

    per_half = width // depth

    def gradient(array, chunk):
        at = pl.ds(pl.multiple_of((chunk % per_half) * depth, depth), depth)
        return lax.dot_general(
            array[chunk // per_half, :, :, at].reshape(nodes, depth), gp[...], (((0,), (0,)), ((), ())),
            preferred_element_type=F32)

    dests = [dest_order(step, pair, pairs) for step in range(pairs)]
    for step, dest in enumerate(dests):
        chunk = 2 * dest + 1 - side
        xs[step, :depth, :] = gradient(full, chunk).astype(BF16)
        xs[step, depth:, :] = gradient(agg, chunk).astype(BF16)
        send(None, lambda step=step: remote(
            xs.at[step], xr.at[step], x_send.at[step], x_recv.at[step], {"rows": partner}))
    for step, dest in enumerate(dests):
        chunk = 2 * dest + side
        part[step, :depth, :] = gradient(full, chunk)
        part[step, depth:, :] = gradient(agg, chunk)
    for step, dest in enumerate(dests):
        arrived(xr.at[step], x_recv.at[step])
        part[step] = part[step] + xr[step].astype(F32)
        if step < pairs - 1:
            way = jnp.where(dest > pair, 0, 1)
            upstream = jnp.where(dest > pair, has_down.astype(jnp.int32), has_up.astype(jnp.int32)) == 1

            @pl.when(upstream)
            def _():
                arrived(zr.at[way, dest], z_recv.at[way, dest])
                part[step] = part[step] + zr[way, dest].astype(F32)

            zs[step] = part[step].astype(BF16)
            send(None, lambda step=step, way=way, dest=dest: remote(
                zs.at[step], zr.at[way, dest], z_send.at[step], z_recv.at[way, dest],
                {"rows": row + 2 - 4 * way}))
        else:
            for way, cond in ((0, has_down), (1, has_up)):
                @pl.when(cond)
                def _():
                    arrived(zr.at[way, pair], z_recv.at[way, pair])
                    part[step] = part[step] + zr[way, pair].astype(F32)
            scale = 1.0 / math.sqrt(nodes * n)
            gs_ref[...] = part[step, :depth, :] * scale
            gn_ref[...] = part[step, depth:, :] * scale

    for cond, make in pending:
        if cond is None:
            make().wait_send()
        else:
            @pl.when(cond)
            def _():
                make().wait_send()


def fused(n, features, edge_vals, block_cols, block_count, w_self, w_neigh, cotangent):
    nodes, width = features.shape
    depth, out_cols = w_self.shape
    blocks, slots = block_cols.shape
    pairs = n // 2
    dma = pltpu.SemaphoreType.DMA
    vmem = pl.BlockSpec(memory_space=pltpu.VMEM)
    smem = pl.BlockSpec(memory_space=pltpu.SMEM)
    flops = 2 * nodes * width * (slots * B + 8 * out_cols)
    return pl.pallas_call(
        functools.partial(layer, n),
        out_shape=(
            jax.ShapeDtypeStruct((nodes, out_cols), BF16),
            jax.ShapeDtypeStruct((depth, out_cols), F32),
            jax.ShapeDtypeStruct((depth, out_cols), F32),
        ),
        in_specs=[vmem, vmem, smem, smem, vmem, vmem, vmem],
        out_specs=(vmem, vmem, vmem),
        scratch_shapes=[
            pltpu.VMEM(((2 * REACH + 1) * blocks, B, width), BF16),
            pltpu.VMEM((2, blocks, B, width), BF16),
            pltpu.VMEM((2, blocks, B, width), BF16),
            pltpu.VMEM((blocks, B, slots * B), BF16),
            pltpu.VMEM((blocks, B, B), F32),
            pltpu.VMEM((2, n * depth, out_cols), BF16),
            pltpu.VMEM((nodes, out_cols), BF16),
            pltpu.VMEM((pairs, 2 * depth, out_cols), F32),
            pltpu.VMEM((pairs, 2 * depth, out_cols), BF16),
            pltpu.VMEM((pairs, 2 * depth, out_cols), BF16),
            pltpu.VMEM((pairs, 2 * depth, out_cols), BF16),
            pltpu.VMEM((2, pairs, 2 * depth, out_cols), BF16),
            dma((2 * REACH + 1, 2)), dma((2,)), dma((2, 2)), dma((2,)),
            dma((2,)), dma((2,)), dma((2, n)), dma((4, n)),
            dma((pairs,)), dma((pairs,)), dma((pairs,)), dma((2, pairs)),
        ],
        compiler_params=pltpu.CompilerParams(
            collective_id=0, has_side_effects=True, vmem_limit_bytes=44 * 2**20,
        ),
        cost_estimate=pl.CostEstimate(
            flops=flops, bytes_accessed=2 * edge_vals.size + 6 * features.size,
            transcendentals=nodes * out_cols,
        ),
    )(features.reshape(blocks, B, width), edge_vals, block_cols, block_count, w_self, w_neigh, cotangent)


def placed_layer(batches, n, cols, *arrays):
    depth = arrays[4].shape[0]
    width = arrays[0].shape[1]
    if batches == 2 and cols == 2 and n % 2 == 0 and depth % TILE == 0 and width % depth == 0:
        return fused(n, *arrays)
    return local(*arrays)


def solution(mesh):
    body = functools.partial(placed_layer, mesh.shape["batch"], mesh.shape["rows"], mesh.shape["cols"])
    placed = (
        P(("batch", "rows"), "cols"),
        P(("batch", "rows"), None, None, None),
        P(("batch", "rows"), None),
        P(("batch", "rows")),
        P("rows", "cols"),
        P("rows", "cols"),
        P(("batch", "rows"), "cols"),
    )
    return jax.shard_map(
        body,
        mesh=mesh,
        in_specs=placed,
        out_specs=(
            P(("batch", "rows"), "cols"),
            P(("batch", "rows"), "cols"),
            P(("batch", "rows"), "cols"),
        ),
        check_vma=False,
    )
```

```python
import functools
import math

import jax
import jax.numpy as jnp
from jax import lax
from jax.experimental import pallas as pl
from jax.experimental.pallas import tpu as pltpu
from jax.sharding import PartitionSpec as P

B = 128
REACH = 2
TILE = 128


def passed_along(array, axis, by):
    peers = lax.axis_size(axis)
    pairs = [(i, i + by) for i in range(peers) if 0 <= i + by < peers]
    return lax.ppermute(array, axis, pairs)


def local(features, edge_vals, block_cols, block_count, w_self, w_neigh, cotangent):
    node_rows = features.shape[0]
    width = features.shape[1]
    blocks_here = node_rows // B
    slot_count = edge_vals.shape[1]
    pieces_list = []
    for offset in range(-REACH, REACH + 1):
        if offset == 0:
            pieces_list.append(features)
        else:
            pieces_list.append(passed_along(features, "rows", -offset))
    extended = jnp.concatenate(pieces_list, axis=0)
    ext_blocks = extended.reshape(-1, B, width)
    base = (lax.axis_index("rows") - REACH) * blocks_here
    local_cols = block_cols - base
    used = jnp.arange(slot_count)[None, :] < block_count[:, None]
    masked = jnp.where(used[:, :, None, None], edge_vals, jnp.zeros_like(edge_vals))
    degree = jnp.sum(masked.astype(jnp.float32), axis=(1, 3))
    picked = ext_blocks[local_cols]
    summed = jnp.einsum("bkij,bkjf->bif", masked, picked, preferred_element_type=jnp.float32)
    aggregated = (summed / degree[:, :, None]).reshape(node_rows, width).astype(jnp.bfloat16)
    full_feat = lax.all_gather(features, "cols", axis=1, tiled=True)
    full_agg = lax.all_gather(aggregated, "cols", axis=1, tiled=True)

    def add_rows(left, piece):
        return jnp.dot(left, piece, preferred_element_type=jnp.float32)

    self_part = add_rows(full_feat, lax.all_gather(w_self, "rows", axis=0, tiled=True))
    neigh_part = add_rows(full_agg, lax.all_gather(w_neigh, "rows", axis=0, tiled=True))
    pre = self_part + neigh_part
    sigma = jax.nn.sigmoid(pre)
    output = (pre * sigma).astype(jnp.bfloat16)
    grad_pre = (cotangent.astype(jnp.float32) * sigma * (1.0 + pre * (1.0 - sigma))).astype(
        jnp.bfloat16
    )
    inverse = 1.0 / math.sqrt(node_rows * lax.axis_size("rows"))
    grads = lax.psum_scatter(
        jnp.concatenate(
            [
                jnp.einsum("nk,nh->kh", full_feat, grad_pre, preferred_element_type=jnp.float32),
                jnp.einsum("nk,nh->kh", full_agg, grad_pre, preferred_element_type=jnp.float32),
            ],
            axis=1,
        ),
        "rows",
        scatter_dimension=0,
        tiled=True,
    )
    out_cols = grad_pre.shape[1]
    grad_self = grads[:, :out_cols] * inverse
    grad_neigh = grads[:, out_cols:] * inverse
    return (output, grad_self, grad_neigh)


F32 = jnp.float32
BF16 = jnp.bfloat16


def dest_order(step, pair, pairs):
    above = pairs - 1 - pair
    low = jnp.where(step < above, pairs - 1 - step, step - above)
    high = jnp.where(step < pair, step, pairs - 1 - (step - pair))
    return jnp.where(step == pairs - 1, pair, jnp.where(2 * pair < pairs, low, high))


def layer(
    n, f_hbm, e_hbm, cols_ref, count_ref, ws_hbm, wn_hbm, cot_hbm,
    out_hbm, grad_ref, e_ref, cot_ref, out_ref,
    ext, full, agg, masked, inv_deg, w, gp, part, xs, xr, zs, zr,
    h_recv, h_x, h_z, h_relay, c_send, c_recv, w_recv, w_send, w_far, here,
    x_send, x_recv, z_send, z_recv,
):
    batch, row, col = lax.axis_index("batch"), lax.axis_index("rows"), lax.axis_index("cols")
    pairs = n // 2
    pair, side = row // 2, row % 2
    partner = row + 1 - 2 * side
    nodes, width = out_ref.shape[0], f_hbm.shape[2]
    depth = ws_hbm.shape[0]
    blocks, slots = e_ref.shape[0], e_ref.shape[1]
    half = blocks // 2
    has_up, has_down = pair < pairs - 1, pair > 0
    pending = []

    def remote(src, dst, send, recv, to):
        return pltpu.make_async_remote_copy(
            src_ref=src, dst_ref=dst, send_sem=send, recv_sem=recv,
            device_id=to, device_id_type=pl.DeviceIdType.MESH,
        )

    def send(cond, make):
        if cond is None:
            make().start()
        else:
            @pl.when(cond)
            def _():
                make().start()
        pending.append((cond, make))

    def arrived(dst, sem):
        remote(dst, dst, sem, sem, {"cols": 1 - col}).wait_recv()

    def shard(which, origin):
        return w.at[which, pl.ds(pl.multiple_of(origin * depth, depth), depth), :]

    own = ext.at[pl.ds(REACH * blocks, blocks)]
    loads = [
        pltpu.make_async_copy(src, dst, here.at[k])
        for k, (src, dst) in enumerate((
            (ws_hbm, shard(0, row)), (wn_hbm, shard(1, row)), (f_hbm, own),
            (e_hbm, e_ref), (f_hbm, full.at[col]), (cot_hbm, cot_ref),
        ))
    ]
    for load in loads:
        load.start()

    barrier = pltpu.get_barrier_semaphore()
    greeted = [{"cols": 1 - col}, {"batch": 1 - batch}, {"rows": partner}]
    greeted += [{"rows": (row + 2 * hop) % n} for hop in range(1, pairs)]
    for to in greeted:
        pl.semaphore_signal(barrier, inc=1, device_id=to, device_id_type=pl.DeviceIdType.MESH)
    for load in loads[:3]:
        load.wait()
    pl.semaphore_wait(barrier, len(greeted))

    def send_w(cond, sem, origin, to):
        send(cond, lambda: remote(
            shard(batch, origin), shard(batch, origin), sem, w_recv.at[batch, origin], to))

    up, down = {"rows": row + 2}, {"rows": row - 2}
    for hop in range(1, pairs):
        send_w(pair + hop < pairs, w_far.at[0, hop], row, {"rows": row + 2 * hop})
        send_w(pair >= hop, w_far.at[1, hop], row, {"rows": row - 2 * hop})
    send_w(None, w_send.at[0, row], row, {"rows": partner})

    def rows_of(slot, piece):
        return ext.at[pl.ds(slot * blocks + piece * half, half)]

    partner_slot = 3 - 2 * side
    diag_slot = 1 + 2 * side
    far_slot = 4 - 4 * side
    for piece in (0, 1):
        send(None, lambda piece=piece: remote(
            rows_of(REACH, piece), rows_of(diag_slot, piece),
            h_x.at[piece], h_recv.at[diag_slot, piece], {"rows": partner}))
        other = 1 - piece
        send(has_up, lambda piece=other: remote(
            rows_of(REACH, piece), rows_of(0, piece),
            h_z.at[0, piece], h_recv.at[0, piece], up))
        send(has_down, lambda piece=other: remote(
            rows_of(REACH, piece), rows_of(4, piece),
            h_z.at[1, piece], h_recv.at[4, piece], down))
    send(None, lambda: remote(
        own, full.at[col], c_send.at[0], c_recv.at[0], {"cols": 1 - col}))

    loads[3].wait()

    def prepare(i, carry):
        degree = jnp.zeros((B, B), F32)
        for s in range(slots):
            keep = jnp.clip(count_ref[i] - s, 0, 1).astype(F32)
            edge = e_ref[i, s].astype(F32) * keep
            masked[i, :, s * B:(s + 1) * B] = edge.astype(BF16)
            degree = degree + edge
        total = jnp.sum(degree, axis=1, keepdims=True)
        inv_deg[i] = jnp.broadcast_to(1.0 / total, (B, B))
        return carry

    lax.fori_loop(0, blocks, prepare, 0)

    def forward(origin, cond):
        @pl.when(cond)
        def _():
            arrived(shard(batch, origin), w_recv.at[batch, origin])
        send_w(cond, w_send.at[0, origin], origin, {"rows": partner})
        send_w(cond, w_send.at[1, origin], origin, {"batch": 1 - batch})

    def hand_over(origin, cond):
        def wait():
            arrived(shard(batch, origin), w_recv.at[batch, origin])
        if cond is None:
            wait()
        else:
            pl.when(cond)(wait)
        send_w(cond, w_send.at[1, origin], origin, {"batch": 1 - batch})

    has_far = jnp.where(side == 0, has_up.astype(jnp.int32), has_down.astype(jnp.int32)) == 1
    has_diag = jnp.where(side == 0, has_down.astype(jnp.int32), has_up.astype(jnp.int32)) == 1
    far = row + 2 - 4 * side
    for hop in range(1, pairs):
        forward(row - 2 * hop, pair >= hop)
        forward(row + 2 * hop, pair + hop < pairs)
        if hop == 1:
            hand_over(partner, None)
    arrived(rows_of(partner_slot, 0), h_recv.at[partner_slot, 0])
    send(has_far, lambda: remote(
        rows_of(partner_slot, 0), rows_of(diag_slot, 0),
        h_relay.at[0], h_recv.at[diag_slot, 0], {"rows": far}))

    @pl.when(has_far)
    def _():
        arrived(rows_of(far_slot, 1), h_recv.at[far_slot, 1])
    send(has_far, lambda: remote(
        rows_of(far_slot, 1), rows_of(partner_slot, 1),
        h_relay.at[1], h_recv.at[partner_slot, 1], {"rows": partner}))
    for hop in range(1, pairs):
        hand_over(partner - 2 * hop, pair >= hop)
        hand_over(partner + 2 * hop, pair + hop < pairs)

    arrived(rows_of(partner_slot, 1), h_recv.at[partner_slot, 1])

    @pl.when(has_far)
    def _():
        arrived(rows_of(far_slot, 0), h_recv.at[far_slot, 0])

    @pl.when(has_diag)
    def _():
        for piece in (0, 1):
            arrived(rows_of(4 - far_slot, piece), h_recv.at[4 - far_slot, piece])
            arrived(rows_of(diag_slot, piece), h_recv.at[diag_slot, piece])

    first = (row - REACH) * blocks

    def aggregate(i, carry):
        acc = jnp.zeros((B, width), F32)
        for s in range(0, slots, 2):
            picked = []
            for k in (s, s + 1):
                picked.append(ext[jnp.clip(cols_ref[i, k] - first, 0, ext.shape[0] - 1)])
            acc = acc + jnp.dot(
                masked[i, :, s * B:(s + 2) * B], jnp.concatenate(picked, axis=0),
                preferred_element_type=F32)
        agg[col, i] = (acc * inv_deg[i, :, 0:1]).astype(BF16)
        return carry

    lax.fori_loop(0, blocks, aggregate, 0)
    send(None, lambda: remote(
        agg.at[col], agg.at[col], c_send.at[1], c_recv.at[1], {"cols": 1 - col}))

    arrived(full.at[1 - col], c_recv.at[0])

    def handed_over(cond, origin):
        def wait():
            arrived(shard(1 - batch, origin), w_recv.at[1 - batch, origin])
        if cond is None:
            wait()
        else:
            pl.when(cond)(wait)

    handed_over(None, partner)
    for hop in range(1, pairs):
        for origin in (row, partner):
            handed_over(pair >= hop, origin - 2 * hop)
            handed_over(pair + hop < pairs, origin + 2 * hop)
    arrived(agg.at[1 - col], c_recv.at[1])

    span = 2
    tile = span * B
    for load in loads[4:]:
        load.wait()

    def left(array, h, i):
        return array[h, pl.ds(i * span, span)].reshape(tile, width)

    def activate(i, carry):
        at = pl.ds(pl.multiple_of(i * tile, tile), tile)
        pre = jnp.zeros((tile, w.shape[2]), F32)
        for h in (0, 1):
            pre = pre + jnp.dot(left(full, h, i), w[0, h * width:(h + 1) * width, :], preferred_element_type=F32)
            pre = pre + jnp.dot(left(agg, h, i), w[1, h * width:(h + 1) * width, :], preferred_element_type=F32)
        sigma = jax.nn.sigmoid(pre)
        out_ref[at, :] = (pre * sigma).astype(BF16)
        gp[at, :] = (cot_ref[at, :].astype(F32) * sigma * (1.0 + pre * (1.0 - sigma))).astype(BF16)
        return carry

    lax.fori_loop(0, nodes // tile, activate, 0)
    store = pltpu.make_async_copy(out_ref, out_hbm, here.at[len(loads)])
    store.start()

    per_half = width // depth

    def gradient(array, chunk):
        at = pl.ds(pl.multiple_of((chunk % per_half) * depth, depth), depth)
        return lax.dot_general(
            array[chunk // per_half, :, :, at].reshape(nodes, depth), gp[...], (((0,), (0,)), ((), ())),
            preferred_element_type=F32)

    dests = [dest_order(step, pair, pairs) for step in range(pairs)]
    for step, dest in enumerate(dests):
        chunk = 2 * dest + 1 - side
        xs[step, :depth, :] = gradient(full, chunk).astype(BF16)
        xs[step, depth:, :] = gradient(agg, chunk).astype(BF16)
        send(None, lambda step=step: remote(
            xs.at[step], xr.at[step], x_send.at[step], x_recv.at[step], {"rows": partner}))
    for step, dest in enumerate(dests):
        chunk = 2 * dest + side
        part[step, :depth, :] = gradient(full, chunk)
        part[step, depth:, :] = gradient(agg, chunk)
    for step, dest in enumerate(dests):
        arrived(xr.at[step], x_recv.at[step])
        part[step] = part[step] + xr[step].astype(F32)
        if step < pairs - 1:
            way = jnp.where(dest > pair, 0, 1)
            upstream = jnp.where(dest > pair, has_down.astype(jnp.int32), has_up.astype(jnp.int32)) == 1

            @pl.when(upstream)
            def _():
                arrived(zr.at[way, dest], z_recv.at[way, dest])
                part[step] = part[step] + zr[way, dest].astype(F32)

            zs[step] = part[step].astype(BF16)
            send(None, lambda step=step, way=way, dest=dest: remote(
                zs.at[step], zr.at[way, dest], z_send.at[step], z_recv.at[way, dest],
                {"rows": row + 2 - 4 * way}))
        else:
            for way, cond in ((0, has_down), (1, has_up)):
                @pl.when(cond)
                def _():
                    arrived(zr.at[way, pair], z_recv.at[way, pair])
                    part[step] = part[step] + zr[way, pair].astype(F32)
            grad_ref[...] = part[step]
    store.wait()

    for cond, make in pending:
        if cond is None:
            make().wait_send()
        else:
            @pl.when(cond)
            def _():
                make().wait_send()


def fused(n, features, edge_vals, block_cols, block_count, w_self, w_neigh, cotangent):
    nodes, width = features.shape
    depth, out_cols = w_self.shape
    blocks, slots = block_cols.shape
    pairs = n // 2
    dma = pltpu.SemaphoreType.DMA
    vmem = pl.BlockSpec(memory_space=pltpu.VMEM)
    hbm = pl.BlockSpec(memory_space=pltpu.HBM)
    smem = pl.BlockSpec(memory_space=pltpu.SMEM)
    flops = 2 * nodes * width * (slots * B + 8 * out_cols)
    output, total = pl.pallas_call(
        functools.partial(layer, n),
        out_shape=(
            jax.ShapeDtypeStruct((nodes, out_cols), BF16),
            jax.ShapeDtypeStruct((2 * depth, out_cols), F32),
        ),
        in_specs=[hbm, hbm, smem, smem, hbm, hbm, hbm],
        out_specs=(hbm, vmem),
        scratch_shapes=[
            pltpu.VMEM(edge_vals.shape, BF16),
            pltpu.VMEM((nodes, out_cols), BF16),
            pltpu.VMEM((nodes, out_cols), BF16),
            pltpu.VMEM(((2 * REACH + 1) * blocks, B, width), BF16),
            pltpu.VMEM((2, blocks, B, width), BF16),
            pltpu.VMEM((2, blocks, B, width), BF16),
            pltpu.VMEM((blocks, B, slots * B), BF16),
            pltpu.VMEM((blocks, B, B), F32),
            pltpu.VMEM((2, n * depth, out_cols), BF16),
            pltpu.VMEM((nodes, out_cols), BF16),
            pltpu.VMEM((pairs, 2 * depth, out_cols), F32),
            pltpu.VMEM((pairs, 2 * depth, out_cols), BF16),
            pltpu.VMEM((pairs, 2 * depth, out_cols), BF16),
            pltpu.VMEM((pairs, 2 * depth, out_cols), BF16),
            pltpu.VMEM((2, pairs, 2 * depth, out_cols), BF16),
            dma((2 * REACH + 1, 2)), dma((2,)), dma((2, 2)), dma((2,)),
            dma((2,)), dma((2,)), dma((2, n)), dma((2, n)), dma((2, pairs)), dma((7,)),
            dma((pairs,)), dma((pairs,)), dma((pairs,)), dma((2, pairs)),
        ],
        compiler_params=pltpu.CompilerParams(
            collective_id=0, has_side_effects=True, vmem_limit_bytes=44 * 2**20,
        ),
        cost_estimate=pl.CostEstimate(
            flops=flops, bytes_accessed=2 * edge_vals.size + 6 * features.size,
            transcendentals=nodes * out_cols,
        ),
    )(features.reshape(blocks, B, width), edge_vals, block_cols, block_count, w_self, w_neigh, cotangent)
    scaled = total * (1.0 / math.sqrt(nodes * n))
    return output, scaled[:depth], scaled[depth:]


def placed_layer(batches, n, cols, *arrays):
    depth = arrays[4].shape[0]
    width = arrays[0].shape[1]
    if batches == 2 and cols == 2 and n % 2 == 0 and depth % TILE == 0 and width % depth == 0:
        return fused(n, *arrays)
    return local(*arrays)


def solution(mesh):
    body = functools.partial(placed_layer, mesh.shape["batch"], mesh.shape["rows"], mesh.shape["cols"])
    placed = (
        P(("batch", "rows"), "cols"),
        P(("batch", "rows"), None, None, None),
        P(("batch", "rows"), None),
        P(("batch", "rows")),
        P("rows", "cols"),
        P("rows", "cols"),
        P(("batch", "rows"), "cols"),
    )
    return jax.shard_map(
        body,
        mesh=mesh,
        in_specs=placed,
        out_specs=(
            P(("batch", "rows"), "cols"),
            P(("batch", "rows"), "cols"),
            P(("batch", "rows"), "cols"),
        ),
        check_vma=False,
    )
```

```python
import functools
import math

import jax
import jax.numpy as jnp
from jax import lax
from jax.experimental import pallas as pl
from jax.experimental.pallas import tpu as pltpu
from jax.sharding import PartitionSpec as P

B = 128
REACH = 2
TILE = 128


def passed_along(array, axis, by):
    peers = lax.axis_size(axis)
    pairs = [(i, i + by) for i in range(peers) if 0 <= i + by < peers]
    return lax.ppermute(array, axis, pairs)


def local(features, edge_vals, block_cols, block_count, w_self, w_neigh, cotangent):
    node_rows = features.shape[0]
    width = features.shape[1]
    blocks_here = node_rows // B
    slot_count = edge_vals.shape[1]
    pieces_list = []
    for offset in range(-REACH, REACH + 1):
        if offset == 0:
            pieces_list.append(features)
        else:
            pieces_list.append(passed_along(features, "rows", -offset))
    extended = jnp.concatenate(pieces_list, axis=0)
    ext_blocks = extended.reshape(-1, B, width)
    base = (lax.axis_index("rows") - REACH) * blocks_here
    local_cols = block_cols - base
    used = jnp.arange(slot_count)[None, :] < block_count[:, None]
    masked = jnp.where(used[:, :, None, None], edge_vals, jnp.zeros_like(edge_vals))
    degree = jnp.sum(masked.astype(jnp.float32), axis=(1, 3))
    picked = ext_blocks[local_cols]
    summed = jnp.einsum("bkij,bkjf->bif", masked, picked, preferred_element_type=jnp.float32)
    aggregated = (summed / degree[:, :, None]).reshape(node_rows, width).astype(jnp.bfloat16)
    full_feat = lax.all_gather(features, "cols", axis=1, tiled=True)
    full_agg = lax.all_gather(aggregated, "cols", axis=1, tiled=True)

    def add_rows(left, piece):
        return jnp.dot(left, piece, preferred_element_type=jnp.float32)

    self_part = add_rows(full_feat, lax.all_gather(w_self, "rows", axis=0, tiled=True))
    neigh_part = add_rows(full_agg, lax.all_gather(w_neigh, "rows", axis=0, tiled=True))
    pre = self_part + neigh_part
    sigma = jax.nn.sigmoid(pre)
    output = (pre * sigma).astype(jnp.bfloat16)
    grad_pre = (cotangent.astype(jnp.float32) * sigma * (1.0 + pre * (1.0 - sigma))).astype(
        jnp.bfloat16
    )
    inverse = 1.0 / math.sqrt(node_rows * lax.axis_size("rows"))
    grads = lax.psum_scatter(
        jnp.concatenate(
            [
                jnp.einsum("nk,nh->kh", full_feat, grad_pre, preferred_element_type=jnp.float32),
                jnp.einsum("nk,nh->kh", full_agg, grad_pre, preferred_element_type=jnp.float32),
            ],
            axis=1,
        ),
        "rows",
        scatter_dimension=0,
        tiled=True,
    )
    out_cols = grad_pre.shape[1]
    grad_self = grads[:, :out_cols] * inverse
    grad_neigh = grads[:, out_cols:] * inverse
    return (output, grad_self, grad_neigh)


F32 = jnp.float32
BF16 = jnp.bfloat16


def dest_order(step, pair, pairs):
    above = pairs - 1 - pair
    low = jnp.where(step < above, pairs - 1 - step, step - above)
    high = jnp.where(step < pair, step, pairs - 1 - (step - pair))
    return jnp.where(step == pairs - 1, pair, jnp.where(2 * pair < pairs, low, high))


def layer(
    n, f_hbm, e_hbm, cols_ref, count_ref, ws_hbm, wn_hbm, cot_hbm,
    out_hbm, grad_ref, e_ref, cot_ref, out_ref,
    ext, full, agg, masked, inv_deg, w, gp, part, xs, xr, zs, zr,
    h_recv, h_x, h_z, h_relay, c_send, c_recv, w_recv, w_send, w_far, here,
    x_send, x_recv, z_send, z_recv,
):
    batch, row, col = lax.axis_index("batch"), lax.axis_index("rows"), lax.axis_index("cols")
    pairs = n // 2
    pair, side = row // 2, row % 2
    partner = row + 1 - 2 * side
    nodes, width = out_ref.shape[0], f_hbm.shape[2]
    depth = ws_hbm.shape[0]
    blocks, slots = e_ref.shape[0], e_ref.shape[1]
    half = blocks // 2
    has_up, has_down = pair < pairs - 1, pair > 0
    pending = []

    def remote(src, dst, send, recv, to):
        return pltpu.make_async_remote_copy(
            src_ref=src, dst_ref=dst, send_sem=send, recv_sem=recv,
            device_id=to, device_id_type=pl.DeviceIdType.MESH,
        )

    def send(cond, make):
        if cond is None:
            make().start()
        else:
            @pl.when(cond)
            def _():
                make().start()
        pending.append((cond, make))

    def arrived(dst, sem):
        remote(dst, dst, sem, sem, {"cols": 1 - col}).wait_recv()

    def shard(which, origin):
        return w.at[which, pl.ds(pl.multiple_of(origin * depth, depth), depth), :]

    own = ext.at[pl.ds(REACH * blocks, blocks)]
    loads = [
        pltpu.make_async_copy(src, dst, here.at[k])
        for k, (src, dst) in enumerate((
            (ws_hbm, shard(0, row)), (wn_hbm, shard(1, row)), (f_hbm, own),
            (e_hbm, e_ref), (f_hbm, full.at[col]), (cot_hbm, cot_ref),
        ))
    ]
    for load in loads:
        load.start()

    barrier = pltpu.get_barrier_semaphore()
    greeted = [{"cols": 1 - col}, {"batch": 1 - batch}, {"rows": partner}]
    greeted += [{"rows": (row + 2 * hop) % n} for hop in range(1, pairs)]
    for to in greeted:
        pl.semaphore_signal(barrier, inc=1, device_id=to, device_id_type=pl.DeviceIdType.MESH)
    for load in loads[:3]:
        load.wait()
    pl.semaphore_wait(barrier, len(greeted))

    def send_w(cond, sem, origin, to):
        send(cond, lambda: remote(
            shard(batch, origin), shard(batch, origin), sem, w_recv.at[batch, origin], to))

    up, down = {"rows": row + 2}, {"rows": row - 2}
    for hop in range(1, pairs):
        send_w(pair + hop < pairs, w_far.at[0, hop], row, {"rows": row + 2 * hop})
        send_w(pair >= hop, w_far.at[1, hop], row, {"rows": row - 2 * hop})
    send_w(None, w_send.at[0, row], row, {"rows": partner})

    def rows_of(slot, piece):
        return ext.at[pl.ds(slot * blocks + piece * half, half)]

    partner_slot = 3 - 2 * side
    diag_slot = 1 + 2 * side
    far_slot = 4 - 4 * side

    def send_x(piece):
        send(None, lambda: remote(
            rows_of(REACH, piece), rows_of(diag_slot, piece),
            h_x.at[piece], h_recv.at[diag_slot, piece], {"rows": partner}))

    send_x(0)
    for piece in (1, 0):
        send(has_up, lambda piece=piece: remote(
            rows_of(REACH, piece), rows_of(0, piece),
            h_z.at[0, piece], h_recv.at[0, piece], up))
        send(has_down, lambda piece=piece: remote(
            rows_of(REACH, piece), rows_of(4, piece),
            h_z.at[1, piece], h_recv.at[4, piece], down))
    send(None, lambda: remote(
        own, full.at[col], c_send.at[0], c_recv.at[0], {"cols": 1 - col}))

    loads[3].wait()

    def prepare(i, carry):
        degree = jnp.zeros((B, B), F32)
        for s in range(slots):
            keep = jnp.clip(count_ref[i] - s, 0, 1).astype(F32)
            edge = e_ref[i, s].astype(F32) * keep
            masked[i, :, s * B:(s + 1) * B] = edge.astype(BF16)
            degree = degree + edge
        total = jnp.sum(degree, axis=1, keepdims=True)
        inv_deg[i] = jnp.broadcast_to(1.0 / total, (B, B))
        return carry

    lax.fori_loop(0, blocks, prepare, 0)

    def forward(origin, cond):
        @pl.when(cond)
        def _():
            arrived(shard(batch, origin), w_recv.at[batch, origin])
        send_w(cond, w_send.at[0, origin], origin, {"rows": partner})
        send_w(cond, w_send.at[1, origin], origin, {"batch": 1 - batch})

    def hand_over(origin, cond):
        def wait():
            arrived(shard(batch, origin), w_recv.at[batch, origin])
        if cond is None:
            wait()
        else:
            pl.when(cond)(wait)
        send_w(cond, w_send.at[1, origin], origin, {"batch": 1 - batch})

    has_far = jnp.where(side == 0, has_up.astype(jnp.int32), has_down.astype(jnp.int32)) == 1
    has_diag = jnp.where(side == 0, has_down.astype(jnp.int32), has_up.astype(jnp.int32)) == 1
    far = row + 2 - 4 * side
    for hop in range(1, pairs):
        forward(row - 2 * hop, pair >= hop)
        forward(row + 2 * hop, pair + hop < pairs)
        if hop == 1:
            hand_over(partner, None)
    send_x(1)
    arrived(rows_of(partner_slot, 0), h_recv.at[partner_slot, 0])
    send(has_far, lambda: remote(
        rows_of(partner_slot, 0), rows_of(diag_slot, 0),
        h_relay.at[0], h_recv.at[diag_slot, 0], {"rows": far}))

    @pl.when(has_far)
    def _():
        arrived(rows_of(far_slot, 1), h_recv.at[far_slot, 1])
    send(has_far, lambda: remote(
        rows_of(far_slot, 1), rows_of(partner_slot, 1),
        h_relay.at[1], h_recv.at[partner_slot, 1], {"rows": partner}))
    for hop in range(1, pairs):
        hand_over(partner - 2 * hop, pair >= hop)
        hand_over(partner + 2 * hop, pair + hop < pairs)

    arrived(rows_of(partner_slot, 1), h_recv.at[partner_slot, 1])

    @pl.when(has_far)
    def _():
        arrived(rows_of(far_slot, 0), h_recv.at[far_slot, 0])

    @pl.when(has_diag)
    def _():
        for piece in (0, 1):
            arrived(rows_of(4 - far_slot, piece), h_recv.at[4 - far_slot, piece])
            arrived(rows_of(diag_slot, piece), h_recv.at[diag_slot, piece])

    first = (row - REACH) * blocks

    def aggregate(i, carry):
        acc = jnp.zeros((B, width), F32)
        for s in range(0, slots, 2):
            picked = []
            for k in (s, s + 1):
                picked.append(ext[jnp.clip(cols_ref[i, k] - first, 0, ext.shape[0] - 1)])
            acc = acc + jnp.dot(
                masked[i, :, s * B:(s + 2) * B], jnp.concatenate(picked, axis=0),
                preferred_element_type=F32)
        agg[col, i] = (acc * inv_deg[i, :, 0:1]).astype(BF16)
        return carry

    lax.fori_loop(0, blocks, aggregate, 0)
    send(None, lambda: remote(
        agg.at[col], agg.at[col], c_send.at[1], c_recv.at[1], {"cols": 1 - col}))

    arrived(full.at[1 - col], c_recv.at[0])

    def handed_over(cond, origin):
        def wait():
            arrived(shard(1 - batch, origin), w_recv.at[1 - batch, origin])
        if cond is None:
            wait()
        else:
            pl.when(cond)(wait)

    handed_over(None, partner)
    for hop in range(1, pairs):
        for origin in (row, partner):
            handed_over(pair >= hop, origin - 2 * hop)
            handed_over(pair + hop < pairs, origin + 2 * hop)
    arrived(agg.at[1 - col], c_recv.at[1])

    span = 2
    tile = span * B
    for load in loads[4:]:
        load.wait()

    def left(array, h, i):
        return array[h, pl.ds(i * span, span)].reshape(tile, width)

    def activate(i, carry):
        at = pl.ds(pl.multiple_of(i * tile, tile), tile)
        pre = jnp.zeros((tile, w.shape[2]), F32)
        for h in (0, 1):
            pre = pre + jnp.dot(left(full, h, i), w[0, h * width:(h + 1) * width, :], preferred_element_type=F32)
            pre = pre + jnp.dot(left(agg, h, i), w[1, h * width:(h + 1) * width, :], preferred_element_type=F32)
        sigma = jax.nn.sigmoid(pre)
        out_ref[at, :] = (pre * sigma).astype(BF16)
        gp[at, :] = (cot_ref[at, :].astype(F32) * sigma * (1.0 + pre * (1.0 - sigma))).astype(BF16)
        return carry

    lax.fori_loop(0, nodes // tile, activate, 0)
    store = pltpu.make_async_copy(out_ref, out_hbm, here.at[len(loads)])
    store.start()

    per_half = width // depth

    def gradient(array, chunk):
        at = pl.ds(pl.multiple_of((chunk % per_half) * depth, depth), depth)
        return lax.dot_general(
            array[chunk // per_half, :, :, at].reshape(nodes, depth), gp[...], (((0,), (0,)), ((), ())),
            preferred_element_type=F32)

    dests = [dest_order(step, pair, pairs) for step in range(pairs)]
    for step, dest in enumerate(dests):
        chunk = 2 * dest + 1 - side
        xs[step, :depth, :] = gradient(full, chunk).astype(BF16)
        xs[step, depth:, :] = gradient(agg, chunk).astype(BF16)
        send(None, lambda step=step: remote(
            xs.at[step], xr.at[step], x_send.at[step], x_recv.at[step], {"rows": partner}))
    for step, dest in enumerate(dests):
        chunk = 2 * dest + side
        part[step, :depth, :] = gradient(full, chunk)
        part[step, depth:, :] = gradient(agg, chunk)
    for step, dest in enumerate(dests):
        arrived(xr.at[step], x_recv.at[step])
        part[step] = part[step] + xr[step].astype(F32)
        if step < pairs - 1:
            way = jnp.where(dest > pair, 0, 1)
            upstream = jnp.where(dest > pair, has_down.astype(jnp.int32), has_up.astype(jnp.int32)) == 1

            @pl.when(upstream)
            def _():
                arrived(zr.at[way, dest], z_recv.at[way, dest])
                part[step] = part[step] + zr[way, dest].astype(F32)

            zs[step] = part[step].astype(BF16)
            send(None, lambda step=step, way=way, dest=dest: remote(
                zs.at[step], zr.at[way, dest], z_send.at[step], z_recv.at[way, dest],
                {"rows": row + 2 - 4 * way}))
        else:
            for way, cond in ((0, has_down), (1, has_up)):
                @pl.when(cond)
                def _():
                    arrived(zr.at[way, pair], z_recv.at[way, pair])
                    part[step] = part[step] + zr[way, pair].astype(F32)
            grad_ref[...] = part[step]
    store.wait()

    for cond, make in pending:
        if cond is None:
            make().wait_send()
        else:
            @pl.when(cond)
            def _():
                make().wait_send()


def fused(n, features, edge_vals, block_cols, block_count, w_self, w_neigh, cotangent):
    nodes, width = features.shape
    depth, out_cols = w_self.shape
    blocks, slots = block_cols.shape
    pairs = n // 2
    dma = pltpu.SemaphoreType.DMA
    vmem = pl.BlockSpec(memory_space=pltpu.VMEM)
    hbm = pl.BlockSpec(memory_space=pltpu.HBM)
    smem = pl.BlockSpec(memory_space=pltpu.SMEM)
    flops = 2 * nodes * width * (slots * B + 8 * out_cols)
    output, total = pl.pallas_call(
        functools.partial(layer, n),
        out_shape=(
            jax.ShapeDtypeStruct((nodes, out_cols), BF16),
            jax.ShapeDtypeStruct((2 * depth, out_cols), F32),
        ),
        in_specs=[hbm, hbm, smem, smem, hbm, hbm, hbm],
        out_specs=(hbm, vmem),
        scratch_shapes=[
            pltpu.VMEM(edge_vals.shape, BF16),
            pltpu.VMEM((nodes, out_cols), BF16),
            pltpu.VMEM((nodes, out_cols), BF16),
            pltpu.VMEM(((2 * REACH + 1) * blocks, B, width), BF16),
            pltpu.VMEM((2, blocks, B, width), BF16),
            pltpu.VMEM((2, blocks, B, width), BF16),
            pltpu.VMEM((blocks, B, slots * B), BF16),
            pltpu.VMEM((blocks, B, B), F32),
            pltpu.VMEM((2, n * depth, out_cols), BF16),
            pltpu.VMEM((nodes, out_cols), BF16),
            pltpu.VMEM((pairs, 2 * depth, out_cols), F32),
            pltpu.VMEM((pairs, 2 * depth, out_cols), BF16),
            pltpu.VMEM((pairs, 2 * depth, out_cols), BF16),
            pltpu.VMEM((pairs, 2 * depth, out_cols), BF16),
            pltpu.VMEM((2, pairs, 2 * depth, out_cols), BF16),
            dma((2 * REACH + 1, 2)), dma((2,)), dma((2, 2)), dma((2,)),
            dma((2,)), dma((2,)), dma((2, n)), dma((2, n)), dma((2, pairs)), dma((7,)),
            dma((pairs,)), dma((pairs,)), dma((pairs,)), dma((2, pairs)),
        ],
        compiler_params=pltpu.CompilerParams(
            collective_id=0, has_side_effects=True, vmem_limit_bytes=63 * 2**20,
        ),
        cost_estimate=pl.CostEstimate(
            flops=flops, bytes_accessed=2 * edge_vals.size + 6 * features.size,
            transcendentals=nodes * out_cols,
        ),
    )(features.reshape(blocks, B, width), edge_vals, block_cols, block_count, w_self, w_neigh, cotangent)
    scale = 1.0 / math.sqrt(nodes * n)
    return output, total[:depth] * scale, total[depth:] * scale


def placed_layer(batches, n, cols, *arrays):
    depth = arrays[4].shape[0]
    width = arrays[0].shape[1]
    if batches == 2 and cols == 2 and n % 2 == 0 and depth % TILE == 0 and width % depth == 0:
        return fused(n, *arrays)
    return local(*arrays)


def solution(mesh):
    body = functools.partial(placed_layer, mesh.shape["batch"], mesh.shape["rows"], mesh.shape["cols"])
    placed = (
        P(("batch", "rows"), "cols"),
        P(("batch", "rows"), None, None, None),
        P(("batch", "rows"), None),
        P(("batch", "rows")),
        P("rows", "cols"),
        P("rows", "cols"),
        P(("batch", "rows"), "cols"),
    )
    return jax.shard_map(
        body,
        mesh=mesh,
        in_specs=placed,
        out_specs=(
            P(("batch", "rows"), "cols"),
            P(("batch", "rows"), "cols"),
            P(("batch", "rows"), "cols"),
        ),
        check_vma=False,
    )
```

```python
import functools
import math

import jax
import jax.numpy as jnp
from jax import lax
from jax.experimental import pallas as pl
from jax.experimental.pallas import tpu as pltpu
from jax.sharding import PartitionSpec as P

B = 128
REACH = 2
TILE = 128


def passed_along(array, axis, by):
    peers = lax.axis_size(axis)
    pairs = [(i, i + by) for i in range(peers) if 0 <= i + by < peers]
    return lax.ppermute(array, axis, pairs)


def local(features, edge_vals, block_cols, block_count, w_self, w_neigh, cotangent):
    node_rows = features.shape[0]
    width = features.shape[1]
    blocks_here = node_rows // B
    slot_count = edge_vals.shape[1]
    pieces_list = []
    for offset in range(-REACH, REACH + 1):
        if offset == 0:
            pieces_list.append(features)
        else:
            pieces_list.append(passed_along(features, "rows", -offset))
    extended = jnp.concatenate(pieces_list, axis=0)
    ext_blocks = extended.reshape(-1, B, width)
    base = (lax.axis_index("rows") - REACH) * blocks_here
    local_cols = block_cols - base
    used = jnp.arange(slot_count)[None, :] < block_count[:, None]
    masked = jnp.where(used[:, :, None, None], edge_vals, jnp.zeros_like(edge_vals))
    degree = jnp.sum(masked.astype(jnp.float32), axis=(1, 3))
    picked = ext_blocks[local_cols]
    summed = jnp.einsum("bkij,bkjf->bif", masked, picked, preferred_element_type=jnp.float32)
    aggregated = (summed / degree[:, :, None]).reshape(node_rows, width).astype(jnp.bfloat16)
    full_feat = lax.all_gather(features, "cols", axis=1, tiled=True)
    full_agg = lax.all_gather(aggregated, "cols", axis=1, tiled=True)

    def add_rows(left, piece):
        return jnp.dot(left, piece, preferred_element_type=jnp.float32)

    self_part = add_rows(full_feat, lax.all_gather(w_self, "rows", axis=0, tiled=True))
    neigh_part = add_rows(full_agg, lax.all_gather(w_neigh, "rows", axis=0, tiled=True))
    pre = self_part + neigh_part
    sigma = jax.nn.sigmoid(pre)
    output = (pre * sigma).astype(jnp.bfloat16)
    grad_pre = (cotangent.astype(jnp.float32) * sigma * (1.0 + pre * (1.0 - sigma))).astype(
        jnp.bfloat16
    )
    inverse = 1.0 / math.sqrt(node_rows * lax.axis_size("rows"))
    grads = lax.psum_scatter(
        jnp.concatenate(
            [
                jnp.einsum("nk,nh->kh", full_feat, grad_pre, preferred_element_type=jnp.float32),
                jnp.einsum("nk,nh->kh", full_agg, grad_pre, preferred_element_type=jnp.float32),
            ],
            axis=1,
        ),
        "rows",
        scatter_dimension=0,
        tiled=True,
    )
    out_cols = grad_pre.shape[1]
    grad_self = grads[:, :out_cols] * inverse
    grad_neigh = grads[:, out_cols:] * inverse
    return (output, grad_self, grad_neigh)


F32 = jnp.float32
BF16 = jnp.bfloat16


def dest_order(step, pair, pairs):
    above = pairs - 1 - pair
    low = jnp.where(step < above, pairs - 1 - step, step - above)
    high = jnp.where(step < pair, step, pairs - 1 - (step - pair))
    return jnp.where(step == pairs - 1, pair, jnp.where(2 * pair < pairs, low, high))


def layer(
    n, f_hbm, e_hbm, cols_ref, count_ref, ws_hbm, wn_hbm, cot_hbm,
    out_hbm, grad_ref, e_ref, cot_ref, out_ref,
    ext, full, agg, masked, inv_deg, w, gp, part, xs, xr, zs, zr,
    h_recv, h_x, h_z, h_relay, c_send, c_recv, w_recv, w_send, w_far, here,
    x_send, x_recv, z_send, z_recv,
):
    batch, row, col = lax.axis_index("batch"), lax.axis_index("rows"), lax.axis_index("cols")
    pairs = n // 2
    pair, side = row // 2, row % 2
    partner = row + 1 - 2 * side
    nodes, width = out_ref.shape[0], f_hbm.shape[2]
    depth = ws_hbm.shape[0]
    blocks, slots = e_ref.shape[0], e_ref.shape[1]
    half = blocks // 2
    has_up, has_down = pair < pairs - 1, pair > 0
    pending = []

    def remote(src, dst, send, recv, to):
        return pltpu.make_async_remote_copy(
            src_ref=src, dst_ref=dst, send_sem=send, recv_sem=recv,
            device_id=to, device_id_type=pl.DeviceIdType.MESH,
        )

    def send(cond, make):
        if cond is None:
            make().start()
        else:
            @pl.when(cond)
            def _():
                make().start()
        pending.append((cond, make))

    def arrived(dst, sem):
        remote(dst, dst, sem, sem, {"cols": 1 - col}).wait_recv()

    def shard(which, origin):
        return w.at[which, pl.ds(pl.multiple_of(origin * depth, depth), depth), :]

    own = ext.at[pl.ds(REACH * blocks, blocks)]
    loads = [
        pltpu.make_async_copy(src, dst, here.at[k])
        for k, (src, dst) in enumerate((
            (ws_hbm, shard(0, row)), (wn_hbm, shard(1, row)), (f_hbm, own),
            (e_hbm, e_ref), (f_hbm, full.at[col]), (cot_hbm, cot_ref),
        ))
    ]
    for load in loads:
        load.start()

    barrier = pltpu.get_barrier_semaphore()
    greeted = [{"cols": 1 - col}, {"batch": 1 - batch}, {"rows": partner}]
    greeted += [{"rows": (row + 2 * hop) % n} for hop in range(1, pairs)]
    for to in greeted:
        pl.semaphore_signal(barrier, inc=1, device_id=to, device_id_type=pl.DeviceIdType.MESH)
    for load in loads[:3]:
        load.wait()
    pl.semaphore_wait(barrier, len(greeted))

    def send_w(cond, sem, origin, to):
        send(cond, lambda: remote(
            shard(batch, origin), shard(batch, origin), sem, w_recv.at[batch, origin], to))

    up, down = {"rows": row + 2}, {"rows": row - 2}
    for hop in range(1, pairs):
        send_w(pair + hop < pairs, w_far.at[0, hop], row, {"rows": row + 2 * hop})
        send_w(pair >= hop, w_far.at[1, hop], row, {"rows": row - 2 * hop})
    send_w(None, w_send.at[0, row], row, {"rows": partner})

    def rows_of(slot, piece):
        return ext.at[pl.ds(slot * blocks + piece * half, half)]

    partner_slot = 3 - 2 * side
    diag_slot = 1 + 2 * side
    far_slot = 4 - 4 * side

    def send_x(piece):
        send(None, lambda: remote(
            rows_of(REACH, piece), rows_of(diag_slot, piece),
            h_x.at[piece], h_recv.at[diag_slot, piece], {"rows": partner}))

    send_x(0)
    for piece in (1, 0):
        send(has_up, lambda piece=piece: remote(
            rows_of(REACH, piece), rows_of(0, piece),
            h_z.at[0, piece], h_recv.at[0, piece], up))
        send(has_down, lambda piece=piece: remote(
            rows_of(REACH, piece), rows_of(4, piece),
            h_z.at[1, piece], h_recv.at[4, piece], down))
    send(None, lambda: remote(
        own, full.at[col], c_send.at[0], c_recv.at[0], {"cols": 1 - col}))

    loads[3].wait()

    def prepare(i, carry):
        degree = jnp.zeros((B, B), F32)
        for s in range(slots):
            keep = jnp.clip(count_ref[i] - s, 0, 1).astype(F32)
            edge = e_ref[i, s].astype(F32) * keep
            masked[i, :, s * B:(s + 1) * B] = edge.astype(BF16)
            degree = degree + edge
        total = jnp.sum(degree, axis=1, keepdims=True)
        inv_deg[i] = jnp.broadcast_to(1.0 / total, (B, B))
        return carry

    lax.fori_loop(0, blocks, prepare, 0)

    def forward(origin, cond):
        @pl.when(cond)
        def _():
            arrived(shard(batch, origin), w_recv.at[batch, origin])
        send_w(cond, w_send.at[0, origin], origin, {"rows": partner})
        send_w(cond, w_send.at[1, origin], origin, {"batch": 1 - batch})

    def hand_over(origin, cond):
        def wait():
            arrived(shard(batch, origin), w_recv.at[batch, origin])
        if cond is None:
            wait()
        else:
            pl.when(cond)(wait)
        send_w(cond, w_send.at[1, origin], origin, {"batch": 1 - batch})

    has_far = jnp.where(side == 0, has_up.astype(jnp.int32), has_down.astype(jnp.int32)) == 1
    has_diag = jnp.where(side == 0, has_down.astype(jnp.int32), has_up.astype(jnp.int32)) == 1
    far = row + 2 - 4 * side
    for hop in range(1, pairs):
        forward(row - 2 * hop, pair >= hop)
        forward(row + 2 * hop, pair + hop < pairs)
        if hop == 1:
            hand_over(partner, None)
    send_x(1)
    arrived(rows_of(partner_slot, 0), h_recv.at[partner_slot, 0])
    send(has_far, lambda: remote(
        rows_of(partner_slot, 0), rows_of(diag_slot, 0),
        h_relay.at[0], h_recv.at[diag_slot, 0], {"rows": far}))

    @pl.when(has_far)
    def _():
        arrived(rows_of(far_slot, 1), h_recv.at[far_slot, 1])
    send(has_far, lambda: remote(
        rows_of(far_slot, 1), rows_of(partner_slot, 1),
        h_relay.at[1], h_recv.at[partner_slot, 1], {"rows": partner}))
    for hop in range(1, pairs):
        hand_over(partner - 2 * hop, pair >= hop)
        hand_over(partner + 2 * hop, pair + hop < pairs)

    arrived(rows_of(partner_slot, 1), h_recv.at[partner_slot, 1])

    @pl.when(has_far)
    def _():
        arrived(rows_of(far_slot, 0), h_recv.at[far_slot, 0])

    @pl.when(has_diag)
    def _():
        for piece in (0, 1):
            arrived(rows_of(4 - far_slot, piece), h_recv.at[4 - far_slot, piece])
            arrived(rows_of(diag_slot, piece), h_recv.at[diag_slot, piece])

    first = (row - REACH) * blocks

    def aggregate(i, carry):
        acc = jnp.zeros((B, width), F32)
        for s in range(0, slots, 2):
            picked = []
            for k in (s, s + 1):
                picked.append(ext[jnp.clip(cols_ref[i, k] - first, 0, ext.shape[0] - 1)])
            acc = acc + jnp.dot(
                masked[i, :, s * B:(s + 2) * B], jnp.concatenate(picked, axis=0),
                preferred_element_type=F32)
        agg[col, i] = (acc * inv_deg[i, :, 0:1]).astype(BF16)
        return carry

    lax.fori_loop(0, blocks, aggregate, 0)
    send(None, lambda: remote(
        agg.at[col], agg.at[col], c_send.at[1], c_recv.at[1], {"cols": 1 - col}))

    arrived(full.at[1 - col], c_recv.at[0])

    def handed_over(cond, origin):
        def wait():
            arrived(shard(1 - batch, origin), w_recv.at[1 - batch, origin])
        if cond is None:
            wait()
        else:
            pl.when(cond)(wait)

    handed_over(None, partner)
    for hop in range(1, pairs):
        for origin in (row, partner):
            handed_over(pair >= hop, origin - 2 * hop)
            handed_over(pair + hop < pairs, origin + 2 * hop)
    arrived(agg.at[1 - col], c_recv.at[1])

    span = 2
    tile = span * B
    for load in loads[4:]:
        load.wait()

    def left(array, h, i):
        return array[h, pl.ds(i * span, span)].reshape(tile, width)

    def activate(i, carry):
        at = pl.ds(pl.multiple_of(i * tile, tile), tile)
        pre = jnp.zeros((tile, w.shape[2]), F32)
        for h in (0, 1):
            pre = pre + jnp.dot(left(full, h, i), w[0, h * width:(h + 1) * width, :], preferred_element_type=F32)
            pre = pre + jnp.dot(left(agg, h, i), w[1, h * width:(h + 1) * width, :], preferred_element_type=F32)
        sigma = jax.nn.sigmoid(pre)
        out_ref[at, :] = (pre * sigma).astype(BF16)
        gp[at, :] = (cot_ref[at, :].astype(F32) * sigma * (1.0 + pre * (1.0 - sigma))).astype(BF16)
        return carry

    lax.fori_loop(0, nodes // tile, activate, 0)
    store = pltpu.make_async_copy(out_ref, out_hbm, here.at[len(loads)])
    store.start()

    per_half = width // depth

    def gradient(array, chunk):
        at = pl.ds(pl.multiple_of((chunk % per_half) * depth, depth), depth)
        return lax.dot_general(
            array[chunk // per_half, :, :, at].reshape(nodes, depth), gp[...], (((0,), (0,)), ((), ())),
            preferred_element_type=F32)

    dests = [dest_order(step, pair, pairs) for step in range(pairs)]
    terms = [(step, dest, k) for step, dest in enumerate(dests) for k in (0, 1)]
    for step, dest, k in terms:
        xs[step, k] = gradient((full, agg)[k], 2 * dest + 1 - side).astype(BF16)
        send(None, lambda step=step, k=k: remote(
            xs.at[step, k], xr.at[step, k], x_send.at[step, k], x_recv.at[step, k],
            {"rows": partner}))
    for step, dest, k in terms:
        part[step, k] = gradient((full, agg)[k], 2 * dest + side)
    for step, dest, k in terms:
        arrived(xr.at[step, k], x_recv.at[step, k])
        part[step, k] = part[step, k] + xr[step, k].astype(F32)
        if step < pairs - 1:
            way = jnp.where(dest > pair, 0, 1)
            upstream = jnp.where(dest > pair, has_down.astype(jnp.int32), has_up.astype(jnp.int32)) == 1

            @pl.when(upstream)
            def _():
                arrived(zr.at[way, dest, k], z_recv.at[way, dest, k])
                part[step, k] = part[step, k] + zr[way, dest, k].astype(F32)

            zs[step, k] = part[step, k].astype(BF16)
            send(None, lambda step=step, way=way, dest=dest, k=k: remote(
                zs.at[step, k], zr.at[way, dest, k], z_send.at[step, k], z_recv.at[way, dest, k],
                {"rows": row + 2 - 4 * way}))
        else:
            for way, cond in ((0, has_down), (1, has_up)):
                @pl.when(cond)
                def _():
                    arrived(zr.at[way, pair, k], z_recv.at[way, pair, k])
                    part[step, k] = part[step, k] + zr[way, pair, k].astype(F32)
            grad_ref[k * depth:(k + 1) * depth, :] = part[step, k]
    store.wait()

    for cond, make in pending:
        if cond is None:
            make().wait_send()
        else:
            @pl.when(cond)
            def _():
                make().wait_send()


def fused(n, features, edge_vals, block_cols, block_count, w_self, w_neigh, cotangent):
    nodes, width = features.shape
    depth, out_cols = w_self.shape
    blocks, slots = block_cols.shape
    pairs = n // 2
    dma = pltpu.SemaphoreType.DMA
    vmem = pl.BlockSpec(memory_space=pltpu.VMEM)
    hbm = pl.BlockSpec(memory_space=pltpu.HBM)
    smem = pl.BlockSpec(memory_space=pltpu.SMEM)
    flops = 2 * nodes * width * (slots * B + 8 * out_cols)
    output, total = pl.pallas_call(
        functools.partial(layer, n),
        out_shape=(
            jax.ShapeDtypeStruct((nodes, out_cols), BF16),
            jax.ShapeDtypeStruct((2 * depth, out_cols), F32),
        ),
        in_specs=[hbm, hbm, smem, smem, hbm, hbm, hbm],
        out_specs=(hbm, vmem),
        scratch_shapes=[
            pltpu.VMEM(edge_vals.shape, BF16),
            pltpu.VMEM((nodes, out_cols), BF16),
            pltpu.VMEM((nodes, out_cols), BF16),
            pltpu.VMEM(((2 * REACH + 1) * blocks, B, width), BF16),
            pltpu.VMEM((2, blocks, B, width), BF16),
            pltpu.VMEM((2, blocks, B, width), BF16),
            pltpu.VMEM((blocks, B, slots * B), BF16),
            pltpu.VMEM((blocks, B, B), F32),
            pltpu.VMEM((2, n * depth, out_cols), BF16),
            pltpu.VMEM((nodes, out_cols), BF16),
            pltpu.VMEM((pairs, 2, depth, out_cols), F32),
            pltpu.VMEM((pairs, 2, depth, out_cols), BF16),
            pltpu.VMEM((pairs, 2, depth, out_cols), BF16),
            pltpu.VMEM((pairs, 2, depth, out_cols), BF16),
            pltpu.VMEM((2, pairs, 2, depth, out_cols), BF16),
            dma((2 * REACH + 1, 2)), dma((2,)), dma((2, 2)), dma((2,)),
            dma((2,)), dma((2,)), dma((2, n)), dma((2, n)), dma((2, pairs)), dma((7,)),
            dma((pairs, 2)), dma((pairs, 2)), dma((pairs, 2)), dma((2, pairs, 2)),
        ],
        compiler_params=pltpu.CompilerParams(
            collective_id=0, has_side_effects=True, vmem_limit_bytes=63 * 2**20,
        ),
        cost_estimate=pl.CostEstimate(
            flops=flops, bytes_accessed=2 * edge_vals.size + 6 * features.size,
            transcendentals=nodes * out_cols,
        ),
    )(features.reshape(blocks, B, width), edge_vals, block_cols, block_count, w_self, w_neigh, cotangent)
    scale = 1.0 / math.sqrt(nodes * n)
    return output, total[:depth] * scale, total[depth:] * scale


def placed_layer(batches, n, cols, *arrays):
    depth = arrays[4].shape[0]
    width = arrays[0].shape[1]
    if batches == 2 and cols == 2 and n % 2 == 0 and depth % TILE == 0 and width % depth == 0:
        return fused(n, *arrays)
    return local(*arrays)


def solution(mesh):
    body = functools.partial(placed_layer, mesh.shape["batch"], mesh.shape["rows"], mesh.shape["cols"])
    placed = (
        P(("batch", "rows"), "cols"),
        P(("batch", "rows"), None, None, None),
        P(("batch", "rows"), None),
        P(("batch", "rows")),
        P("rows", "cols"),
        P("rows", "cols"),
        P(("batch", "rows"), "cols"),
    )
    return jax.shard_map(
        body,
        mesh=mesh,
        in_specs=placed,
        out_specs=(
            P(("batch", "rows"), "cols"),
            P(("batch", "rows"), "cols"),
            P(("batch", "rows"), "cols"),
        ),
        check_vma=False,
    )
```

```python
import functools
import math

import jax
import jax.numpy as jnp
from jax import lax
from jax.experimental import pallas as pl
from jax.experimental.pallas import tpu as pltpu
from jax.sharding import PartitionSpec as P

B = 128
REACH = 2
TILE = 128
SHARES = 2


def passed_along(array, axis, by):
    peers = lax.axis_size(axis)
    pairs = [(i, i + by) for i in range(peers) if 0 <= i + by < peers]
    return lax.ppermute(array, axis, pairs)


def local(features, edge_vals, block_cols, block_count, w_self, w_neigh, cotangent):
    node_rows = features.shape[0]
    width = features.shape[1]
    blocks_here = node_rows // B
    slot_count = edge_vals.shape[1]
    pieces_list = []
    for offset in range(-REACH, REACH + 1):
        if offset == 0:
            pieces_list.append(features)
        else:
            pieces_list.append(passed_along(features, "rows", -offset))
    extended = jnp.concatenate(pieces_list, axis=0)
    ext_blocks = extended.reshape(-1, B, width)
    base = (lax.axis_index("rows") - REACH) * blocks_here
    local_cols = block_cols - base
    used = jnp.arange(slot_count)[None, :] < block_count[:, None]
    masked = jnp.where(used[:, :, None, None], edge_vals, jnp.zeros_like(edge_vals))
    degree = jnp.sum(masked.astype(jnp.float32), axis=(1, 3))
    picked = ext_blocks[local_cols]
    summed = jnp.einsum("bkij,bkjf->bif", masked, picked, preferred_element_type=jnp.float32)
    aggregated = (summed / degree[:, :, None]).reshape(node_rows, width).astype(jnp.bfloat16)
    full_feat = lax.all_gather(features, "cols", axis=1, tiled=True)
    full_agg = lax.all_gather(aggregated, "cols", axis=1, tiled=True)

    def add_rows(left, piece):
        return jnp.dot(left, piece, preferred_element_type=jnp.float32)

    self_part = add_rows(full_feat, lax.all_gather(w_self, "rows", axis=0, tiled=True))
    neigh_part = add_rows(full_agg, lax.all_gather(w_neigh, "rows", axis=0, tiled=True))
    pre = self_part + neigh_part
    sigma = jax.nn.sigmoid(pre)
    output = (pre * sigma).astype(jnp.bfloat16)
    grad_pre = (cotangent.astype(jnp.float32) * sigma * (1.0 + pre * (1.0 - sigma))).astype(
        jnp.bfloat16
    )
    inverse = 1.0 / math.sqrt(node_rows * lax.axis_size("rows"))
    grads = lax.psum_scatter(
        jnp.concatenate(
            [
                jnp.einsum("nk,nh->kh", full_feat, grad_pre, preferred_element_type=jnp.float32),
                jnp.einsum("nk,nh->kh", full_agg, grad_pre, preferred_element_type=jnp.float32),
            ],
            axis=1,
        ),
        "rows",
        scatter_dimension=0,
        tiled=True,
    )
    out_cols = grad_pre.shape[1]
    grad_self = grads[:, :out_cols] * inverse
    grad_neigh = grads[:, out_cols:] * inverse
    return (output, grad_self, grad_neigh)


F32 = jnp.float32
BF16 = jnp.bfloat16


def dest_order(step, pair, pairs):
    above = pairs - 1 - pair
    low = jnp.where(step < above, pairs - 1 - step, step - above)
    high = jnp.where(step < pair, step, pairs - 1 - (step - pair))
    return jnp.where(step == pairs - 1, pair, jnp.where(2 * pair < pairs, low, high))


def layer(
    n, f_hbm, e_hbm, cols_ref, count_ref, ws_hbm, wn_hbm, cot_hbm,
    out_hbm, grad_ref, e_ref, cot_ref, out_ref,
    ext, full, agg, masked, inv_deg, w, gp, part, xs, xr, zs, zr,
    h_recv, h_x, h_z, h_relay, c_send, c_recv, w_recv, w_send, w_far, here,
    x_send, x_recv, z_send, z_recv,
):
    batch, row, col = lax.axis_index("batch"), lax.axis_index("rows"), lax.axis_index("cols")
    pairs = n // 2
    pair, side = row // 2, row % 2
    partner = row + 1 - 2 * side
    nodes, width = out_ref.shape[0], f_hbm.shape[2]
    depth = ws_hbm.shape[0]
    blocks, slots = e_ref.shape[0], e_ref.shape[1]
    half = blocks // 2
    has_up, has_down = pair < pairs - 1, pair > 0
    pending = []

    def remote(src, dst, send, recv, to):
        return pltpu.make_async_remote_copy(
            src_ref=src, dst_ref=dst, send_sem=send, recv_sem=recv,
            device_id=to, device_id_type=pl.DeviceIdType.MESH,
        )

    def send(cond, make):
        if cond is None:
            make().start()
        else:
            @pl.when(cond)
            def _():
                make().start()
        pending.append((cond, make))

    def arrived(dst, sem):
        remote(dst, dst, sem, sem, {"cols": 1 - col}).wait_recv()

    def shard(which, origin):
        return w.at[which, pl.ds(pl.multiple_of(origin * depth, depth), depth), :]

    own = ext.at[pl.ds(REACH * blocks, blocks)]
    loads = [
        pltpu.make_async_copy(src, dst, here.at[k])
        for k, (src, dst) in enumerate((
            (ws_hbm, shard(0, row)), (wn_hbm, shard(1, row)), (f_hbm, own),
            (e_hbm, e_ref), (f_hbm, full.at[col]), (cot_hbm, cot_ref),
        ))
    ]
    for load in loads:
        load.start()

    barrier = pltpu.get_barrier_semaphore()
    greeted = [{"cols": 1 - col}, {"batch": 1 - batch}, {"rows": partner}]
    greeted += [{"rows": (row + 2 * hop) % n} for hop in range(1, pairs)]
    for to in greeted:
        pl.semaphore_signal(barrier, inc=1, device_id=to, device_id_type=pl.DeviceIdType.MESH)
    for load in loads[:3]:
        load.wait()
    pl.semaphore_wait(barrier, len(greeted))

    def send_w(cond, sem, origin, to):
        send(cond, lambda: remote(
            shard(batch, origin), shard(batch, origin), sem, w_recv.at[batch, origin], to))

    up, down = {"rows": row + 2}, {"rows": row - 2}
    for hop in range(1, pairs):
        send_w(pair + hop < pairs, w_far.at[0, hop], row, {"rows": row + 2 * hop})
        send_w(pair >= hop, w_far.at[1, hop], row, {"rows": row - 2 * hop})
    send_w(None, w_send.at[0, row], row, {"rows": partner})

    def rows_of(slot, piece):
        return ext.at[pl.ds(slot * blocks + piece * half, half)]

    partner_slot = 3 - 2 * side
    diag_slot = 1 + 2 * side
    far_slot = 4 - 4 * side

    def send_x(piece):
        send(None, lambda: remote(
            rows_of(REACH, piece), rows_of(diag_slot, piece),
            h_x.at[piece], h_recv.at[diag_slot, piece], {"rows": partner}))

    send_x(0)
    for piece in (1, 0):
        send(has_up, lambda piece=piece: remote(
            rows_of(REACH, piece), rows_of(0, piece),
            h_z.at[0, piece], h_recv.at[0, piece], up))
        send(has_down, lambda piece=piece: remote(
            rows_of(REACH, piece), rows_of(4, piece),
            h_z.at[1, piece], h_recv.at[4, piece], down))
    send(None, lambda: remote(
        own, full.at[col], c_send.at[0], c_recv.at[0], {"cols": 1 - col}))

    loads[3].wait()

    def prepare(i, carry):
        degree = jnp.zeros((B, B), F32)
        for s in range(slots):
            keep = jnp.clip(count_ref[i] - s, 0, 1).astype(F32)
            edge = e_ref[i, s].astype(F32) * keep
            masked[i, :, s * B:(s + 1) * B] = edge.astype(BF16)
            degree = degree + edge
        total = jnp.sum(degree, axis=1, keepdims=True)
        inv_deg[i] = jnp.broadcast_to(1.0 / total, (B, B))
        return carry

    lax.fori_loop(0, blocks, prepare, 0)

    def forward(origin, cond):
        @pl.when(cond)
        def _():
            arrived(shard(batch, origin), w_recv.at[batch, origin])
        send_w(cond, w_send.at[0, origin], origin, {"rows": partner})
        send_w(cond, w_send.at[1, origin], origin, {"batch": 1 - batch})

    def hand_over(origin, cond):
        def wait():
            arrived(shard(batch, origin), w_recv.at[batch, origin])
        if cond is None:
            wait()
        else:
            pl.when(cond)(wait)
        send_w(cond, w_send.at[1, origin], origin, {"batch": 1 - batch})

    has_far = jnp.where(side == 0, has_up.astype(jnp.int32), has_down.astype(jnp.int32)) == 1
    has_diag = jnp.where(side == 0, has_down.astype(jnp.int32), has_up.astype(jnp.int32)) == 1
    far = row + 2 - 4 * side
    for hop in range(1, pairs):
        forward(row - 2 * hop, pair >= hop)
        forward(row + 2 * hop, pair + hop < pairs)
        if hop == 1:
            hand_over(partner, None)
    send_x(1)
    arrived(rows_of(partner_slot, 0), h_recv.at[partner_slot, 0])
    send(has_far, lambda: remote(
        rows_of(partner_slot, 0), rows_of(diag_slot, 0),
        h_relay.at[0], h_recv.at[diag_slot, 0], {"rows": far}))

    @pl.when(has_far)
    def _():
        arrived(rows_of(far_slot, 1), h_recv.at[far_slot, 1])
    send(has_far, lambda: remote(
        rows_of(far_slot, 1), rows_of(partner_slot, 1),
        h_relay.at[1], h_recv.at[partner_slot, 1], {"rows": partner}))
    for hop in range(1, pairs):
        hand_over(partner - 2 * hop, pair >= hop)
        hand_over(partner + 2 * hop, pair + hop < pairs)

    arrived(rows_of(partner_slot, 1), h_recv.at[partner_slot, 1])

    @pl.when(has_far)
    def _():
        arrived(rows_of(far_slot, 0), h_recv.at[far_slot, 0])

    @pl.when(has_diag)
    def _():
        for piece in (0, 1):
            arrived(rows_of(4 - far_slot, piece), h_recv.at[4 - far_slot, piece])
            arrived(rows_of(diag_slot, piece), h_recv.at[diag_slot, piece])

    first = (row - REACH) * blocks

    def aggregate(i, carry):
        acc = jnp.zeros((B, width), F32)
        for s in range(0, slots, 2):
            picked = []
            for k in (s, s + 1):
                picked.append(ext[jnp.clip(cols_ref[i, k] - first, 0, ext.shape[0] - 1)])
            acc = acc + jnp.dot(
                masked[i, :, s * B:(s + 2) * B], jnp.concatenate(picked, axis=0),
                preferred_element_type=F32)
        agg[col, i] = (acc * inv_deg[i, :, 0:1]).astype(BF16)
        return carry

    lax.fori_loop(0, blocks, aggregate, 0)
    send(None, lambda: remote(
        agg.at[col], agg.at[col], c_send.at[1], c_recv.at[1], {"cols": 1 - col}))

    arrived(full.at[1 - col], c_recv.at[0])

    def handed_over(cond, origin):
        def wait():
            arrived(shard(1 - batch, origin), w_recv.at[1 - batch, origin])
        if cond is None:
            wait()
        else:
            pl.when(cond)(wait)

    handed_over(None, partner)
    for hop in range(1, pairs):
        for origin in (row, partner):
            handed_over(pair >= hop, origin - 2 * hop)
            handed_over(pair + hop < pairs, origin + 2 * hop)
    arrived(agg.at[1 - col], c_recv.at[1])

    span = 2
    tile = span * B
    for load in loads[4:]:
        load.wait()

    def left(array, h, i):
        return array[h, pl.ds(i * span, span)].reshape(tile, width)

    def activate(i, carry):
        at = pl.ds(pl.multiple_of(i * tile, tile), tile)
        pre = jnp.zeros((tile, w.shape[2]), F32)
        for h in (0, 1):
            pre = pre + jnp.dot(left(full, h, i), w[0, h * width:(h + 1) * width, :], preferred_element_type=F32)
            pre = pre + jnp.dot(left(agg, h, i), w[1, h * width:(h + 1) * width, :], preferred_element_type=F32)
        sigma = jax.nn.sigmoid(pre)
        out_ref[at, :] = (pre * sigma).astype(BF16)
        gp[at, :] = (cot_ref[at, :].astype(F32) * sigma * (1.0 + pre * (1.0 - sigma))).astype(BF16)
        return carry

    lax.fori_loop(0, nodes // tile, activate, 0)
    store = pltpu.make_async_copy(out_ref, out_hbm, here.at[len(loads)])
    store.start()

    per_half = width // depth

    def gradient(array, chunk):
        at = pl.ds(pl.multiple_of((chunk % per_half) * depth, depth), depth)
        return lax.dot_general(
            array[chunk // per_half, :, :, at].reshape(nodes, depth), gp[...], (((0,), (0,)), ((), ())),
            preferred_element_type=F32)

    dests = [dest_order(step, pair, pairs) for step in range(pairs)]
    terms = [(step, dest, k) for step, dest in enumerate(dests) for k in range(2 * SHARES)]
    share = depth // SHARES
    for step, dest, k in terms:
        if k % SHARES == 0:
            whole = gradient((full, agg)[k // SHARES], 2 * dest + 1 - side).astype(BF16)
        at = k % SHARES * share
        xs[step, k] = whole[at:at + share, :]
        send(None, lambda step=step, k=k: remote(
            xs.at[step, k], xr.at[step, k], x_send.at[step, k], x_recv.at[step, k],
            {"rows": partner}))
    for step, dest, k in terms:
        if k % SHARES == 0:
            whole = gradient((full, agg)[k // SHARES], 2 * dest + side)
        at = k % SHARES * share
        part[step, k] = whole[at:at + share, :]
    for step, dest, k in terms:
        arrived(xr.at[step, k], x_recv.at[step, k])
        part[step, k] = part[step, k] + xr[step, k].astype(F32)
        if step < pairs - 1:
            way = jnp.where(dest > pair, 0, 1)
            upstream = jnp.where(dest > pair, has_down.astype(jnp.int32), has_up.astype(jnp.int32)) == 1

            @pl.when(upstream)
            def _():
                arrived(zr.at[way, dest, k], z_recv.at[way, dest, k])
                part[step, k] = part[step, k] + zr[way, dest, k].astype(F32)

            zs[step, k] = part[step, k].astype(BF16)
            send(None, lambda step=step, way=way, dest=dest, k=k: remote(
                zs.at[step, k], zr.at[way, dest, k], z_send.at[step, k], z_recv.at[way, dest, k],
                {"rows": row + 2 - 4 * way}))
        else:
            for way, cond in ((0, has_down), (1, has_up)):
                @pl.when(cond)
                def _():
                    arrived(zr.at[way, pair, k], z_recv.at[way, pair, k])
                    part[step, k] = part[step, k] + zr[way, pair, k].astype(F32)
            grad_ref[k * share:(k + 1) * share, :] = part[step, k]
    store.wait()

    for cond, make in pending:
        if cond is None:
            make().wait_send()
        else:
            @pl.when(cond)
            def _():
                make().wait_send()


def fused(n, features, edge_vals, block_cols, block_count, w_self, w_neigh, cotangent):
    nodes, width = features.shape
    depth, out_cols = w_self.shape
    blocks, slots = block_cols.shape
    pairs = n // 2
    dma = pltpu.SemaphoreType.DMA
    vmem = pl.BlockSpec(memory_space=pltpu.VMEM)
    hbm = pl.BlockSpec(memory_space=pltpu.HBM)
    smem = pl.BlockSpec(memory_space=pltpu.SMEM)
    flops = 2 * nodes * width * (slots * B + 8 * out_cols)
    output, total = pl.pallas_call(
        functools.partial(layer, n),
        out_shape=(
            jax.ShapeDtypeStruct((nodes, out_cols), BF16),
            jax.ShapeDtypeStruct((2 * depth, out_cols), F32),
        ),
        in_specs=[hbm, hbm, smem, smem, hbm, hbm, hbm],
        out_specs=(hbm, vmem),
        scratch_shapes=[
            pltpu.VMEM(edge_vals.shape, BF16),
            pltpu.VMEM((nodes, out_cols), BF16),
            pltpu.VMEM((nodes, out_cols), BF16),
            pltpu.VMEM(((2 * REACH + 1) * blocks, B, width), BF16),
            pltpu.VMEM((2, blocks, B, width), BF16),
            pltpu.VMEM((2, blocks, B, width), BF16),
            pltpu.VMEM((blocks, B, slots * B), BF16),
            pltpu.VMEM((blocks, B, B), F32),
            pltpu.VMEM((2, n * depth, out_cols), BF16),
            pltpu.VMEM((nodes, out_cols), BF16),
            pltpu.VMEM((pairs, 2 * SHARES, depth // SHARES, out_cols), F32),
            pltpu.VMEM((pairs, 2 * SHARES, depth // SHARES, out_cols), BF16),
            pltpu.VMEM((pairs, 2 * SHARES, depth // SHARES, out_cols), BF16),
            pltpu.VMEM((pairs, 2 * SHARES, depth // SHARES, out_cols), BF16),
            pltpu.VMEM((2, pairs, 2 * SHARES, depth // SHARES, out_cols), BF16),
            dma((2 * REACH + 1, 2)), dma((2,)), dma((2, 2)), dma((2,)),
            dma((2,)), dma((2,)), dma((2, n)), dma((2, n)), dma((2, pairs)), dma((7,)),
            dma((pairs, 2 * SHARES)), dma((pairs, 2 * SHARES)), dma((pairs, 2 * SHARES)),
            dma((2, pairs, 2 * SHARES)),
        ],
        compiler_params=pltpu.CompilerParams(
            collective_id=0, has_side_effects=True, vmem_limit_bytes=63 * 2**20,
        ),
        cost_estimate=pl.CostEstimate(
            flops=flops, bytes_accessed=2 * edge_vals.size + 6 * features.size,
            transcendentals=nodes * out_cols,
        ),
    )(features.reshape(blocks, B, width), edge_vals, block_cols, block_count, w_self, w_neigh, cotangent)
    scale = 1.0 / math.sqrt(nodes * n)
    return output, total[:depth] * scale, total[depth:] * scale


def placed_layer(batches, n, cols, *arrays):
    depth = arrays[4].shape[0]
    width = arrays[0].shape[1]
    if batches == 2 and cols == 2 and n % 2 == 0 and depth % TILE == 0 and width % depth == 0:
        return fused(n, *arrays)
    return local(*arrays)


def solution(mesh):
    body = functools.partial(placed_layer, mesh.shape["batch"], mesh.shape["rows"], mesh.shape["cols"])
    placed = (
        P(("batch", "rows"), "cols"),
        P(("batch", "rows"), None, None, None),
        P(("batch", "rows"), None),
        P(("batch", "rows")),
        P("rows", "cols"),
        P("rows", "cols"),
        P(("batch", "rows"), "cols"),
    )
    return jax.shard_map(
        body,
        mesh=mesh,
        in_specs=placed,
        out_specs=(
            P(("batch", "rows"), "cols"),
            P(("batch", "rows"), "cols"),
            P(("batch", "rows"), "cols"),
        ),
        check_vma=False,
    )
```
